256 devices in a mesh: blk: 64 (over y, z, x_lo), sub: 4 (over x_hi, core).
Axes of the slice: x: 4 (x_hi: 2, x_lo: 2; x = x_hi * 2 + x_lo), y: 4, z: 8, core: 2. Of those that a mesh axis runs over, the one named last changes fastest.
Arguments:
- tile_values: bfloat16 [2, 256, 128, 128, 128], P(None, ('blk', 'sub')), may hold values from -0.1875 to 0.1875
- tile_rows: int32 [2, 256, 128], P(None, ('blk', 'sub')), may hold values from 0 to 15
- tile_cols: int32 [2, 256, 128], P(None, ('blk', 'sub')), may hold values from 0 to 2047
- tile_counts: int32 [2, 256], P(None, ('blk', 'sub')), may hold values from 16 to 128, as said below
- labels: int32 [524288], P(('blk', 'sub')), may hold values from -1 to 1, as said below
- dual_logits: float32 [524288], P(('blk', 'sub')), may hold values from -6 to 6
- weights: float32 [16777216], P('blk'), may hold values from -6 to 6
- adagrad_sums: float32 [16777216], P('blk'), may hold values from 0.05 to 0.5
- section_steps: int32 [2], replicated, may hold values from 1 to 16
Outputs:
- weights_out: float32 [16777216], P('blk')
- adagrad_out: float32 [16777216], P('blk')
- dual_out: float32 [524288], P(('blk', 'sub'))
The draws below stay inside these ranges and needn't reach their ends.
Inputs may be any that keep to these rules, and one draw needn't show every extreme that they name: `tile_counts`: slot k of a shard in a section holds a tile only when k is below its count; in every section some shard's count is 128. `labels`: each label is -1 or +1.
All inputs are finite; a program needn't handle non-finite values.
Results may differ from the reference program's by a relative error of at most 0.00067.
Values may be sent and summed in bfloat16 or wider, within the bound.
A program may use at most 64 MiB of HBM per device.

```python
import math
import jax
import jax.numpy as jnp
from jax import lax

WB = 262144
TILE = 128
CAP = 128
RT = 16
SECTIONS = 2
NBLOCKS = 64
SUBS = 4
SHARDS = 256
CTILES = 2048
ROWS = 524288
FEATURES = 16777216


def draw_tile_counts(key, part):
    key = jax.random.fold_in(key, 11)
    first_key, second_key, third_key = jax.random.split(key, 3)
    first_draw = jax.random.randint(first_key, (SECTIONS, SHARDS), 1, CAP + 1)
    second_draw = jax.random.randint(second_key, (SECTIONS, SHARDS), 1, CAP + 1)
    base_counts = jnp.maximum((CAP + 7) // 8, first_draw * second_draw // CAP)
    busiest = jax.random.randint(third_key, (SECTIONS, 1), 0, SHARDS)
    shard_ids = jnp.arange(SHARDS, dtype=jnp.int32)[None, :]
    return jnp.where(shard_ids == busiest, CAP, base_counts).astype(jnp.int32)


def draw_labels(key, part):
    key = jax.random.fold_in(key, 23)
    return (2 * jax.random.randint(key, (ROWS,), 0, 2) - 1).astype(jnp.int32)


def set_ends(array, stream_key, least, high):
    shape = array.shape
    index_at = [jax.random.randint(jax.random.fold_in(stream_key, axis), (), 0, shape[axis]) for axis in range(len(shape))]
    array = array.at[tuple(index_at)].set(least)
    longest = shape.index(max(shape))
    index_at[longest] = (index_at[longest] + 1) % shape[longest]
    return array.at[tuple(index_at)].set(high)


def levels(rng, shape, pieces, smallest, largest):
    loudness, own = 1.0, jax.random.fold_in(rng, 6)
    for axis_at, parts in pieces:
        draws = jnp.exp(jax.random.uniform(jax.random.fold_in(own, axis_at), (parts,), jnp.float32, smallest / len(pieces), largest / len(pieces)))
        loudness = loudness * jnp.repeat(draws, shape[axis_at] // parts).reshape([-1 if axis == axis_at else 1 for axis in range(len(shape))])
    return loudness


def bell_draw(key, dims, spread, most, cuts=(), kind=jnp.bfloat16):
    array = spread * jax.random.normal(key, dims, jnp.float32)
    if cuts:
        array = array * levels(key, dims, cuts, -0.22, 0.18)
    return jnp.clip(array, -most, most).astype(kind)


def setup_inputs(seed: int = 0) -> dict:
    keys = jax.random.split(jax.random.key(seed), 10)
    tile_values = bell_draw(keys[0], (SECTIONS, SHARDS, CAP, TILE, TILE), (TILE * CAP // RT) ** -0.5, 0.1875, ((1, 256),))
    tile_rows = set_ends(jax.random.randint(keys[1], (SECTIONS, SHARDS, CAP), 0, RT), jax.random.fold_in(keys[1], 1), 0, RT - 1).astype(jnp.int32)
    tile_cols = set_ends(jax.random.randint(keys[2], (SECTIONS, SHARDS, CAP), 0, CTILES), jax.random.fold_in(keys[2], 1), 0, CTILES - 1).astype(jnp.int32)
    tile_counts = draw_tile_counts(jax.random.fold_in(keys[9], 71), 0)
    labels = draw_labels(jax.random.fold_in(keys[9], 71), 0)
    dual_logits = bell_draw(keys[5], (ROWS,), 1.0, 6.0, ((0, 256),), jnp.float32)
    weights = bell_draw(keys[6], (FEATURES,), 1.0, 6.0, ((0, 64),), jnp.float32)
    adagrad_sums = jnp.clip(jnp.exp(math.log(0.5) - 2.3025851 * jax.random.uniform(keys[7], (FEATURES,), jnp.float32) ** levels(keys[7], (FEATURES,), ((0, 64),), -0.2, 0.2)), 0.05, 0.5)
    section_steps = jax.random.randint(keys[8], (SECTIONS,), 1, 17).astype(jnp.int32)
    return {"tile_values": tile_values, "tile_rows": tile_rows, "tile_cols": tile_cols, "tile_counts": tile_counts, "labels": labels, "dual_logits": dual_logits, "weights": weights, "adagrad_sums": adagrad_sums, "section_steps": section_steps}


penalty = 0.1
dual_rate = 0.5
primal_rate = 0.8

def shard_section(tile_block, row_ids, col_ids, filled, label_signs, logits, held_bf16, dual_step):
    tile_size = tile_block.shape[-1]
    active = (jnp.arange(tile_block.shape[0], dtype=jnp.int32) < filled).astype(jnp.float32)
    columns = held_bf16.reshape(-1, tile_size)[col_ids]
    margin_tiles = jnp.einsum('kij,kj->ki', tile_block.astype(jnp.float32), columns.astype(jnp.float32), precision=lax.Precision.HIGHEST) * active[:, None]
    margins = jax.ops.segment_sum(margin_tiles, row_ids, num_segments=logits.shape[0] // tile_size).reshape(-1)
    logits = (1.0 - dual_step) * logits - dual_step * label_signs * margins
    scaled = (jax.nn.sigmoid(logits) * label_signs).astype(jnp.bfloat16).reshape(-1, tile_size)
    backward = jnp.einsum('kij,ki->kj', tile_block.astype(jnp.float32), scaled[row_ids].astype(jnp.float32), precision=lax.Precision.HIGHEST) * active[:, None]
    partial_value = jax.ops.segment_sum(backward, col_ids, num_segments=held_bf16.shape[0] // tile_size)
    return (logits, partial_value.reshape(-1))

def reference(tile_values, tile_rows, tile_cols, tile_counts, labels, dual_logits, weights, adagrad_sums, section_steps):
    held_blocks = weights.reshape(NBLOCKS, WB)
    sum_blocks = adagrad_sums.reshape(NBLOCKS, WB)
    logit_blocks = dual_logits.reshape(NBLOCKS, SUBS, -1)
    sign_blocks = labels.astype(jnp.float32).reshape(NBLOCKS, SUBS, -1)
    zero_index = jnp.zeros((), jnp.int32)
    for section_index in range(SECTIONS):
        steps_now = section_steps[section_index].astype(jnp.float32)
        dual_step = dual_rate / jnp.sqrt(steps_now)
        primal_step = primal_rate / jnp.sqrt(steps_now)
        section_at = jnp.asarray(section_index).astype(jnp.int32)

        def position(inputs):
            where_at, logit_rows, sign_rows, held_row, sum_row = inputs
            held_bf16 = held_row.astype(jnp.bfloat16)
            first_shard = (where_at * SUBS).astype(jnp.int32)
            tile_block = lax.dynamic_slice(tile_values, (section_at, first_shard, zero_index, zero_index, zero_index), (1, SUBS, CAP, TILE, TILE))[0]
            row_block = lax.dynamic_slice(tile_rows, (section_at, first_shard, zero_index), (1, SUBS, CAP))[0]
            col_block = lax.dynamic_slice(tile_cols, (section_at, first_shard, zero_index), (1, SUBS, CAP))[0]
            count_block = lax.dynamic_slice(tile_counts, (section_at, first_shard), (1, SUBS))[0]
            gradient = penalty * held_row
            new_logits = []
            for sub_index in range(SUBS):
                logits, partial_value = shard_section(tile_block[sub_index], row_block[sub_index], col_block[sub_index], count_block[sub_index], sign_rows[sub_index], logit_rows[sub_index], held_bf16, dual_step)
                new_logits.append(logits)
                gradient = gradient + partial_value
            sum_row = sum_row + gradient * gradient
            held_row = held_row - primal_step * gradient / jnp.sqrt(sum_row)
            return (jnp.stack(new_logits), held_row, sum_row)
        logit_blocks, held_blocks, sum_blocks = lax.map(position, (jnp.arange(NBLOCKS, dtype=jnp.int32), logit_blocks, sign_blocks, held_blocks, sum_blocks))
        held_blocks = jnp.roll(held_blocks, 1, axis=0)
        sum_blocks = jnp.roll(sum_blocks, 1, axis=0)
    return (held_blocks.reshape(-1), sum_blocks.reshape(-1), logit_blocks.reshape(-1))
```

```python
import functools

import jax
import jax.numpy as jnp
from jax import lax
from jax.experimental import pallas as pl
from jax.experimental.pallas import tpu as pltpu
from jax.sharding import PartitionSpec as P

MESH = pl.DeviceIdType.MESH
SUBS = 4
SLOTS = 128
TILE = 128
GROUP = 16
GROUPS = SLOTS // GROUP
CTILES = 2048
HALF = CTILES // 2
PARTS = 4
PART = HALF // PARTS
GROWS = SLOTS + 8
OUT_PARTS = 8
OUT_PART = CTILES // OUT_PARTS

PENALTY = 0.1
DUAL_RATE = 0.5
PRIMAL_RATE = 0.8

F32 = jnp.float32
BF16 = jnp.bfloat16


def split_terms(value):
    high = value.astype(BF16)
    low = (value - high.astype(F32)).astype(BF16)
    return jnp.concatenate([high, low], axis=1)


def onehot_sum(match, terms):
    both = jnp.dot(match.astype(F32).astype(BF16), terms, preferred_element_type=F32)
    return both[:, :TILE] + both[:, TILE:]


def kernel(
    n,
    rows_s,
    cols_s,
    counts_s,
    steps_s,
    cols_v,
    labels_v,
    dual_v,
    tiles_h,
    weights_h,
    sums_h,
    weights_out,
    sums_out,
    dual_out,
    tiles,
    weights,
    sums,
    asked_v,
    asked_s,
    answer,
    answered,
    hrows,
    scaled,
    grads,
    near0,
    near1,
    far0,
    old,
    terms0,
    terms1,
    result,
    tile_sem,
    local_sem,
    ask_sem,
    asked_sem,
    answer_sem,
    dense_sem,
    copy_sem,
    grad_send,
    grad_recv,
    out_sem,
):
    p = lax.axis_index("blk")
    q = lax.axis_index("sub")
    core = lax.rem(q, 2)
    twin = q + 1 - 2 * core
    after = lax.rem(p + 1, n)
    after2 = lax.rem(p + 2, n)
    before = lax.rem(p + n - 1, n)
    before2 = lax.rem(p + n - 2, n)

    barrier = pltpu.get_barrier_semaphore()
    for other in range(SUBS):
        pl.semaphore_signal(barrier, inc=1, device_id=(before, other), device_id_type=MESH)
        pl.semaphore_signal(barrier, inc=1, device_id=(before2, other), device_id_type=MESH)
    pl.semaphore_signal(barrier, inc=1, device_id=(after, q), device_id_type=MESH)
    pl.semaphore_signal(barrier, inc=1, device_id=(p, twin), device_id_type=MESH)

    copy_w = pltpu.make_async_copy(weights_h, weights, local_sem.at[0])
    copy_w.start()
    for section in range(2):
        for g in range(GROUPS):
            pltpu.make_async_copy(
                tiles_h.at[section, 0, pl.ds(g * GROUP, GROUP)],
                tiles.at[section, pl.ds(g * GROUP, GROUP)],
                tile_sem.at[section, g],
            ).start()
        if section == 0:
            copy_s = pltpu.make_async_copy(sums_h, sums, local_sem.at[1])
            copy_s.start()

    pl.semaphore_wait(barrier, 2 * SUBS + 2)

    def remote(src, dst, send, recv, device):
        return pltpu.make_async_remote_copy(
            src_ref=src, dst_ref=dst, send_sem=send, recv_sem=recv, device_id=device, device_id_type=MESH
        )

    ask = remote(cols_v.at[1], asked_v, ask_sem.at[0], asked_sem.at[0], (before, q))
    ask.start()

    def dense(part, which):
        source = (weights_h, sums_h)[which]
        at = pl.multiple_of(core * HALF + part * PART, PART)
        return remote(
            source.at[pl.ds(at, PART)],
            old.at[which, pl.ds(at, PART)],
            dense_sem.at[0, which, part],
            dense_sem.at[1, which, part],
            (after2, q),
        )

    def forward_dense(part, which):
        at = pl.multiple_of(core * HALF + part * PART, PART)
        return remote(
            old.at[which, pl.ds(at, PART)],
            old.at[which, pl.ds(at, PART)],
            copy_sem.at[0, which, part],
            copy_sem.at[1, which, part],
            (p, twin),
        )

    for part in range(PARTS):
        for which in range(2):
            dense(part, which).start()

    sub16 = lax.broadcasted_iota(jnp.int32, (GROUP, TILE), 0)

    def section_pass(section, load_h, logits):
        count = counts_s[section]
        base = section * SLOTS

        def forward(g, total):
            pltpu.make_async_copy(
                tiles_h.at[section, 0, pl.ds(g * GROUP, GROUP)],
                tiles.at[section, pl.ds(g * GROUP, GROUP)],
                tile_sem.at[section, g],
            ).wait()
            for j in range(GROUP):
                k = g * GROUP + j
                row = jnp.where(k < count, rows_s[base + k], -1)
                lhs = jnp.where(sub16 == row, load_h(k), 0.0).astype(BF16)
                total = total + lax.dot_general(
                    lhs, tiles[section, k], (((1,), (1,)), ((), ())), preferred_element_type=F32
                )
            return total

        margins = lax.fori_loop(0, GROUPS, forward, jnp.zeros((GROUP, TILE), F32))
        steps = jnp.full((GROUP, TILE), steps_s[section], jnp.int32).astype(F32)
        dual_step = DUAL_RATE / jnp.sqrt(steps)
        signs = labels_v[...].astype(F32)
        logits = (1.0 - dual_step) * logits - dual_step * signs * margins
        scaled[...] = jax.nn.sigmoid(logits) * signs

        def backward(g, carry):
            total = jnp.zeros((GROUP, TILE), F32)
            for j in range(GROUP):
                k = g * GROUP + j
                slot = jnp.where(k < count, j, -1)
                value = scaled[pl.ds(rows_s[base + k], 1), :]
                lhs = jnp.where(sub16 == slot, value, 0.0).astype(BF16)
                total = total + jnp.dot(lhs, tiles[section, k], preferred_element_type=F32)
            grads[section, pl.ds(pl.multiple_of(g * GROUP, GROUP), GROUP), :] = total
            return carry

        lax.fori_loop(0, GROUPS, backward, 0)
        ids = jnp.broadcast_to(cols_v[section].astype(F32), (8, TILE))
        grads[section, pl.ds(SLOTS, 8), :] = ids
        return logits

    def send_grad(kind, other):
        section = (0, 1, 0)[kind]
        target = (near0, near1, far0)[kind]
        place = (after, after, after2)[kind]
        return remote(
            grads.at[section],
            target.at[q],
            grad_send.at[kind, other],
            grad_recv.at[kind, q],
            (place, other),
        )

    def recv_grad(kind, other):
        section = (0, 1, 0)[kind]
        target = (near0, near1, far0)[kind]
        return remote(
            grads.at[section], target.at[other], grad_send.at[kind, other], grad_recv.at[kind, other], (p, twin)
        )

    copy_w.wait()
    logits = section_pass(0, lambda k: weights[pl.ds(cols_s[k], 1), :], dual_v[...])
    for kind in (0, 2):
        for other in range(SUBS):
            send_grad(kind, other).start()

    ask.wait()
    to_scalar = pltpu.make_async_copy(asked_v, asked_s, local_sem.at[2])
    to_scalar.start()
    to_scalar.wait()
    copy_s.wait()

    def gather(g, carry):
        for j in range(GROUP):
            k = g * GROUP + j
            at = asked_s[0, k]
            answer[0, pl.ds(k, 1), :] = weights[pl.ds(at, 1), :]
            answer[1, pl.ds(k, 1), :] = sums[pl.ds(at, 1), :]
        return carry

    lax.fori_loop(0, GROUPS, gather, 0)
    give = remote(answer, answered, answer_sem.at[0], answer_sem.at[1], (after, q))
    give.start()

    def primal(section, shape):
        steps = jnp.full(shape, steps_s[section], jnp.int32).astype(F32)
        return PRIMAL_RATE / jnp.sqrt(steps)

    def fill_terms(terms, source):
        for other in range(SUBS):
            terms[pl.ds(other * SLOTS, SLOTS), :] = split_terms(source[other, :SLOTS, :])

    def lane_ids(source):
        return jnp.concatenate([source[other, SLOTS : SLOTS + 1, :] for other in range(SUBS)], axis=1)

    for other in range(SUBS):
        recv_grad(0, other).wait_recv()
    fill_terms(terms0, near0)
    mine = jnp.transpose(jnp.broadcast_to(cols_v[1].astype(F32), (TILE, TILE)))
    mine = jnp.concatenate([mine] * SUBS, axis=1)
    picked = onehot_sum(mine == lane_ids(near0), terms0[...])
    give.wait_recv()
    gradient = PENALTY * answered[0] + picked
    after_sums = answered[1] + gradient * gradient
    hrows[...] = answered[0] - primal(0, (SLOTS, TILE)) * gradient / jnp.sqrt(after_sums)

    logits = section_pass(1, lambda k: hrows[pl.ds(k, 1), :], logits)
    for other in range(SUBS):
        send_grad(1, other).start()
    dual_out[...] = logits

    for part in range(PARTS):
        for which in range(2):
            dense(part, which).wait_recv()
            forward_dense(part, which).start()
    for other in range(SUBS):
        recv_grad(2, other).wait_recv()
    fill_terms(terms0, far0)
    for other in range(SUBS):
        recv_grad(1, other).wait_recv()
    fill_terms(terms1, near1)
    for part in range(PARTS):
        for which in range(2):
            forward_dense(part, which).wait()

    def finish(part, carry):
        at = pl.multiple_of(part * OUT_PART, OUT_PART)
        ids = (lax.broadcasted_iota(jnp.int32, (OUT_PART, SUBS * SLOTS), 0) + at).astype(F32)
        w = old[0, pl.ds(at, OUT_PART), :]
        s = old[1, pl.ds(at, OUT_PART), :]
        g0 = PENALTY * w + onehot_sum(ids == lane_ids(far0), terms0[...])
        s = s + g0 * g0
        w = w - primal(0, (OUT_PART, TILE)) * g0 / jnp.sqrt(s)
        g1 = PENALTY * w + onehot_sum(ids == lane_ids(near1), terms1[...])
        s = s + g1 * g1
        w = w - primal(1, (OUT_PART, TILE)) * g1 / jnp.sqrt(s)
        result[0, pl.ds(at, OUT_PART), :] = w
        result[1, pl.ds(at, OUT_PART), :] = s
        pltpu.make_async_copy(
            result.at[0, pl.ds(at, OUT_PART)], weights_out.at[pl.ds(at, OUT_PART)], out_sem.at[0, part]
        ).start()
        pltpu.make_async_copy(
            result.at[1, pl.ds(at, OUT_PART)], sums_out.at[pl.ds(at, OUT_PART)], out_sem.at[1, part]
        ).start()
        return carry

    lax.fori_loop(0, OUT_PARTS, finish, 0)

    for part in range(PARTS):
        for which in range(2):
            dense(part, which).wait_send()
    for kind in range(3):
        for other in range(SUBS):
            send_grad(kind, other).wait_send()
    give.wait_send()

    def drain(part, carry):
        at = pl.multiple_of(part * OUT_PART, OUT_PART)
        pltpu.make_async_copy(
            result.at[0, pl.ds(at, OUT_PART)], weights_out.at[pl.ds(at, OUT_PART)], out_sem.at[0, part]
        ).wait()
        pltpu.make_async_copy(
            result.at[1, pl.ds(at, OUT_PART)], sums_out.at[pl.ds(at, OUT_PART)], out_sem.at[1, part]
        ).wait()
        return carry

    lax.fori_loop(0, OUT_PARTS, drain, 0)


def per_device(
    n, tile_values, tile_rows, tile_cols, tile_counts, labels, dual_logits, weights, adagrad_sums, section_steps
):
    any_space = pl.BlockSpec(memory_space=pl.ANY)
    smem = pl.BlockSpec(memory_space=pltpu.SMEM)
    vmem = pl.BlockSpec(memory_space=pltpu.VMEM)
    dma = pltpu.SemaphoreType.DMA
    out = pl.pallas_call(
        functools.partial(kernel, n),
        out_shape=(
            jax.ShapeDtypeStruct((CTILES, TILE), F32),
            jax.ShapeDtypeStruct((CTILES, TILE), F32),
            jax.ShapeDtypeStruct((GROUP, TILE), F32),
        ),
        in_specs=[smem, smem, smem, smem, vmem, vmem, vmem, any_space, any_space, any_space],
        out_specs=(any_space, any_space, vmem),
        scratch_shapes=[
            pltpu.VMEM((2, SLOTS, TILE, TILE), BF16),
            pltpu.VMEM((CTILES, TILE), F32),
            pltpu.VMEM((CTILES, TILE), F32),
            pltpu.VMEM((1, SLOTS), jnp.int32),
            pltpu.SMEM((1, SLOTS), jnp.int32),
            pltpu.VMEM((2, SLOTS, TILE), F32),
            pltpu.VMEM((2, SLOTS, TILE), F32),
            pltpu.VMEM((SLOTS, TILE), F32),
            pltpu.VMEM((GROUP, TILE), F32),
            pltpu.VMEM((2, GROWS, TILE), F32),
            pltpu.VMEM((SUBS, GROWS, TILE), F32),
            pltpu.VMEM((SUBS, GROWS, TILE), F32),
            pltpu.VMEM((SUBS, GROWS, TILE), F32),
            pltpu.VMEM((2, CTILES, TILE), F32),
            pltpu.VMEM((SUBS * SLOTS, 2 * TILE), BF16),
            pltpu.VMEM((SUBS * SLOTS, 2 * TILE), BF16),
            pltpu.VMEM((2, CTILES, TILE), F32),
            dma((2, GROUPS)),
            dma((3,)),
            dma((1,)),
            dma((1,)),
            dma((2,)),
            dma((2, 2, PARTS)),
            dma((2, 2, PARTS)),
            dma((3, SUBS)),
            dma((3, SUBS)),
            dma((2, OUT_PARTS)),
        ],
        compiler_params=pltpu.CompilerParams(
            collective_id=0, has_side_effects=True, vmem_limit_bytes=62 * 1024 * 1024
        ),
        name="descent",
    )(
        tile_rows.reshape(-1),
        tile_cols.reshape(-1),
        tile_counts.reshape(-1),
        section_steps,
        tile_cols,
        labels.reshape(GROUP, TILE),
        dual_logits.reshape(GROUP, TILE),
        tile_values,
        weights.reshape(CTILES, TILE),
        adagrad_sums.reshape(CTILES, TILE),
    )
    return out[0].reshape(-1), out[1].reshape(-1), out[2].reshape(-1)


def solution(mesh):
    in_specs = (
        P(None, ("blk", "sub"), None, None, None),
        P(None, ("blk", "sub"), None),
        P(None, ("blk", "sub"), None),
        P(None, ("blk", "sub")),
        P(("blk", "sub")),
        P(("blk", "sub")),
        P("blk"),
        P("blk"),
        P(),
    )
    out_specs = (P("blk"), P("blk"), P(("blk", "sub")))
    return jax.shard_map(
        functools.partial(per_device, mesh.shape["blk"]),
        mesh=mesh,
        in_specs=in_specs,
        out_specs=out_specs,
        check_vma=False,
    )
```

```python
import functools

import jax
import jax.numpy as jnp
from jax import lax
from jax.experimental import pallas as pl
from jax.experimental.pallas import tpu as pltpu
from jax.sharding import PartitionSpec as P

MESH = pl.DeviceIdType.MESH
SUBS = 4
SLOTS = 128
TILE = 128
GROUP = 16
GROUPS = SLOTS // GROUP
WIDE = 4
CTILES = 2048
QUARTER = CTILES // SUBS
PIECES = 2
PIECE = QUARTER // PIECES
GROWS = SLOTS + 8
CROWS = SLOTS + GROUP
OUT_PARTS = SUBS
OUT_PART = CTILES // OUT_PARTS
LOADS = (4, 2)

PENALTY = 0.1
DUAL_RATE = 0.5
PRIMAL_RATE = 0.8

LEVELS = 32766.0
WEIGHT_CODE = (-25.0, 27.6)
GRADIENT_CODE = (-18.0, 22.7)
SUM_MID = 0.275
SUM_SCALE = 32767.0 / 0.22501

F32 = jnp.float32
BF16 = jnp.bfloat16
I32 = jnp.int32


def encode_log(value, code_range):
    low, span = code_range
    size = jnp.log2(jnp.maximum(jnp.abs(value), 1e-30))
    code = jnp.clip(jnp.round((size - low) * (LEVELS / span)), 0.0, LEVELS)
    return jnp.where(value < 0.0, -code, code).astype(I32).astype(jnp.int16)


def decode_log(code, code_range):
    low, span = code_range
    code = code.astype(I32).astype(F32)
    size = jnp.exp2(jnp.abs(code) * (span / LEVELS) + low)
    return jnp.where(code < 0.0, -size, jnp.where(code > 0.0, size, 0.0))


def encode_sums(value):
    code = jnp.clip(jnp.round((value - SUM_MID) * SUM_SCALE), -32767.0, 32767.0)
    return code.astype(I32).astype(jnp.int16)


def decode_sums(code):
    return code.astype(I32).astype(F32) * (1.0 / SUM_SCALE) + SUM_MID


def split_terms(value):
    high = value.astype(BF16)
    low = (value - high.astype(F32)).astype(BF16)
    return jnp.concatenate([high, low], axis=1)


def onehot_sum(match, terms):
    both = jnp.dot(match.astype(F32).astype(BF16), terms, preferred_element_type=F32)
    return both[:, :TILE] + both[:, TILE:]


def fill_terms(terms, source, coded):
    for other in range(SUBS):
        value = source[other, :SLOTS, :]
        if coded:
            value = decode_log(value, GRADIENT_CODE)
        terms[pl.ds(other * SLOTS, SLOTS), :] = split_terms(value)


def lane_ids(source, coded):
    ids = [source[other, SLOTS:, :] for other in range(SUBS)]
    if coded:
        ids = [value.astype(I32).astype(F32) for value in ids]
    return jnp.concatenate([value[:1, :] for value in ids], axis=1)


def primal_step(steps_s, section, shape):
    steps = jnp.full(shape, steps_s[section], I32).astype(F32)
    return PRIMAL_RATE / jnp.sqrt(steps)


def part_ids(at):
    return (lax.broadcasted_iota(I32, (OUT_PART, SUBS * SLOTS), 0) + at).astype(F32)


def kernel(
    n,
    rows_s,
    cols_s,
    counts_s,
    steps_s,
    cols_v,
    labels_v,
    dual_v,
    tiles_h,
    weights_h,
    sums_h,
    mid_weights,
    mid_sums,
    near1,
    dual_out,
    tiles,
    weights,
    sums,
    asked_v,
    asked_s,
    answer,
    answered,
    hrows,
    scaled,
    grads,
    coded,
    near0,
    far0,
    codes,
    old,
    terms,
    result,
    tile_sem,
    local_sem,
    ask_sem,
    answer_sem,
    dense_send,
    dense_recv,
    grad_send,
    grad_recv,
    out_sem,
):
    p = lax.axis_index("blk")
    q = lax.axis_index("sub")
    twin = q + 1 - 2 * lax.rem(q, 2)
    opp = lax.rem(q + 2, SUBS)
    opptwin = lax.rem(twin + 2, SUBS)
    after = lax.rem(p + 1, n)
    after2 = lax.rem(p + 2, n)
    before = lax.rem(p + n - 1, n)
    before2 = lax.rem(p + n - 2, n)

    barrier = pltpu.get_barrier_semaphore()
    senders = [(before, q), (before, opp), (before2, q), (before2, opp), (after, q), (p, twin), (p, opp)]
    for device in senders:
        pl.semaphore_signal(barrier, inc=1, device_id=device, device_id_type=MESH)

    def tile_copy(section, load):
        size = SLOTS // LOADS[section]
        return pltpu.make_async_copy(
            tiles_h.at[section, 0, pl.ds(load * size, size)],
            tiles.at[section, pl.ds(load * size, size)],
            tile_sem.at[section, load],
        )

    copy_w = pltpu.make_async_copy(weights_h, weights, local_sem.at[0])
    copy_w.start()
    for load in range(LOADS[0]):
        tile_copy(0, load).start()
    copy_s = pltpu.make_async_copy(sums_h, sums, local_sem.at[1])
    copy_s.start()
    for load in range(LOADS[1]):
        tile_copy(1, load).start()

    def remote(src, dst, send, recv, device):
        return pltpu.make_async_remote_copy(
            src_ref=src, dst_ref=dst, send_sem=send, recv_sem=recv, device_id=device, device_id_type=MESH
        )

    sub16 = lax.broadcasted_iota(I32, (GROUP, TILE), 0)

    def forward(section, load_h):
        count = counts_s[section]
        base = section * SLOTS

        def group(g, total):
            for j in range(0, GROUP, WIDE):
                lhs = []
                for i in range(WIDE):
                    k = g * GROUP + j + i
                    row = jnp.where(k < count, rows_s[base + k], -1)
                    lhs.append(jnp.where(sub16 == row, load_h(k), 0.0).astype(BF16))
                rhs = [tiles[section, g * GROUP + j + i] for i in range(WIDE)]
                total = total + lax.dot_general(
                    jnp.concatenate(lhs, axis=1),
                    jnp.concatenate(rhs, axis=1),
                    (((1,), (1,)), ((), ())),
                    preferred_element_type=F32,
                )
            return total

        total = jnp.zeros((GROUP, TILE), F32)
        each = GROUPS // LOADS[section]
        for load in range(LOADS[section]):
            tile_copy(section, load).wait()
            total = lax.fori_loop(load * each, (load + 1) * each, group, total)
        return total

    def new_logits(section, logits, margins):
        steps = jnp.full((GROUP, TILE), steps_s[section], I32).astype(F32)
        dual_step = DUAL_RATE / jnp.sqrt(steps)
        signs = labels_v[...].astype(F32)
        logits = (1.0 - dual_step) * logits - dual_step * signs * margins
        scaled[...] = jax.nn.sigmoid(logits) * signs
        return logits

    def backward(section):
        count = counts_s[section]
        base = section * SLOTS

        def group(g, carry):
            lhs = []
            for j in range(GROUP):
                k = g * GROUP + j
                slot = jnp.where(k < count, j, -1)
                value = scaled[pl.ds(rows_s[base + k], 1), :]
                lhs.append(jnp.where(sub16 == slot, value, 0.0).astype(BF16))
            rhs = tiles[section, pl.ds(g * GROUP, GROUP)].reshape(GROUP * TILE, TILE)
            grads[section, pl.ds(pl.multiple_of(g * GROUP, GROUP), GROUP), :] = jnp.dot(
                jnp.concatenate(lhs, axis=1), rhs, preferred_element_type=F32
            )
            return carry

        lax.fori_loop(0, GROUPS, group, 0)

    ask = remote(cols_v.at[1], asked_v, ask_sem.at[0], ask_sem.at[1], (before, q))

    def dense(stage, piece):
        owner = opp if stage == 3 else q
        to = ((after2, q), (p, opp), (p, twin), (p, twin))[stage]
        src = codes.at[piece] if stage == 0 else old.at[owner, piece]
        return remote(src, old.at[owner, piece], dense_send.at[stage, piece], dense_recv.at[stage, piece], to)

    def dense_arrived(stage, piece):
        ref = old.at[(q, opp, twin, opptwin)[stage], piece]
        remote(ref, ref, dense_send.at[stage, piece], dense_recv.at[stage, piece], (p, twin)).wait_recv()

    def grad(kind, stage, way):
        target = (near0, near1, far0)[kind]
        owner = (q, opp)[way]
        if stage == 0:
            src, slot = (grads.at[0], coded.at[1], coded.at[0])[kind], q
            to = ((after, after, after2)[kind], owner)
        else:
            src, slot = target.at[owner], owner
            to = (p, twin)
        return remote(
            src, target.at[slot], grad_send.at[kind, stage, way], grad_recv.at[kind, stage, way], to
        )

    def grad_arrived(kind, stage, way):
        target = (near0, near1, far0)[kind]
        owner = ((q, opp), (twin, opptwin))[stage][way]
        ref = target.at[owner]
        remote(
            ref, ref, grad_send.at[kind, stage, way], grad_recv.at[kind, stage, way], (p, twin)
        ).wait_recv()

    grads[0, pl.ds(SLOTS, 8), :] = jnp.broadcast_to(cols_v[0].astype(F32), (8, TILE))
    for section in range(2):
        coded[section, pl.ds(SLOTS, GROUP), :] = jnp.broadcast_to(cols_v[section], (GROUP, TILE)).astype(
            jnp.int16
        )

    copy_w.wait()
    margins = forward(0, lambda k: weights[pl.ds(cols_s[k], 1), :])
    logits = new_logits(0, dual_v[...], margins)

    pl.semaphore_wait(barrier, len(senders))
    ask.start()
    backward(0)
    for way in range(2):
        grad(0, 0, way).start()

    copy_s.wait()
    for piece in range(PIECES):
        at = pl.multiple_of(q * QUARTER + piece * PIECE, PIECE)
        codes[piece, 0] = encode_log(weights[pl.ds(at, PIECE), :], WEIGHT_CODE)
        codes[piece, 1] = encode_sums(sums[pl.ds(at, PIECE), :])
    coded[0, :SLOTS, :] = encode_log(grads[0, :SLOTS, :], GRADIENT_CODE)

    ask.wait()
    to_scalar = pltpu.make_async_copy(asked_v, asked_s, local_sem.at[2])
    to_scalar.start()
    to_scalar.wait()

    def gather(g, carry):
        for j in range(GROUP):
            k = g * GROUP + j
            at = asked_s[0, k]
            answer[0, pl.ds(k, 1), :] = weights[pl.ds(at, 1), :]
            answer[1, pl.ds(k, 1), :] = sums[pl.ds(at, 1), :]
        return carry

    lax.fori_loop(0, GROUPS, gather, 0)
    give = remote(answer, answered, answer_sem.at[0], answer_sem.at[1], (after, q))
    give.start()
    for piece in range(PIECES):
        dense(0, piece).start()
    for way in range(2):
        grad(2, 0, way).start()

    mine = jnp.transpose(jnp.broadcast_to(cols_v[1].astype(F32), (TILE, TILE)))
    mine = jnp.concatenate([mine] * SUBS, axis=1)
    for way in range(2):
        grad_arrived(0, 0, way)
        grad(0, 1, way).start()
    give.wait_recv()
    for way in range(2):
        grad_arrived(0, 1, way)
    fill_terms(terms, near0, False)
    picked = onehot_sum(mine == lane_ids(near0, False), terms[...])
    gradient = PENALTY * answered[0] + picked
    after_sums = answered[1] + gradient * gradient
    hrows[...] = answered[0] - primal_step(steps_s, 0, (SLOTS, TILE)) * gradient / jnp.sqrt(after_sums)

    margins = forward(1, lambda k: hrows[pl.ds(k, 1), :])
    logits = new_logits(1, logits, margins)
    dual_out[...] = logits
    dense_arrived(0, 0)
    dense(1, 0).start()
    dense(2, 0).start()
    backward(1)
    coded[1, :SLOTS, :] = encode_log(grads[1, :SLOTS, :], GRADIENT_CODE)
    for way in range(2):
        grad(1, 0, way).start()

    for piece in range(1, PIECES):
        dense_arrived(0, piece)
        dense(1, piece).start()
        dense(2, piece).start()
    for way in range(2):
        grad_arrived(2, 0, way)
        grad(2, 1, way).start()
    dense_arrived(1, 0)
    dense(3, 0).start()
    for way in range(2):
        grad_arrived(2, 1, way)
    fill_terms(terms, far0, True)
    ids0 = lane_ids(far0, True)

    def mid_copy(owner, which):
        at = pl.multiple_of(owner * OUT_PART, OUT_PART)
        return pltpu.make_async_copy(
            result.at[which, pl.ds(at, OUT_PART)],
            (mid_weights, mid_sums)[which].at[pl.ds(at, OUT_PART)],
            out_sem.at[which, owner],
        )

    def section0(owner):
        at = pl.multiple_of(owner * OUT_PART, OUT_PART)
        w = decode_log(old[owner, :, 0].reshape(OUT_PART, TILE), WEIGHT_CODE)
        s = decode_sums(old[owner, :, 1].reshape(OUT_PART, TILE))
        gradient = PENALTY * w + onehot_sum(part_ids(at) == ids0, terms[...])
        s = s + gradient * gradient
        result[0, pl.ds(at, OUT_PART), :] = (
            w - primal_step(steps_s, 0, (OUT_PART, TILE)) * gradient / jnp.sqrt(s)
        )
        result[1, pl.ds(at, OUT_PART), :] = s
        for which in range(2):
            mid_copy(owner, which).start()

    section0(q)
    for piece in range(PIECES):
        dense_arrived(2, piece)
    section0(twin)
    for piece in range(1, PIECES):
        dense_arrived(1, piece)
        dense(3, piece).start()
    for way in range(2):
        grad_arrived(1, 0, way)
        grad(1, 1, way).start()
    section0(opp)
    for piece in range(PIECES):
        dense_arrived(3, piece)
    section0(opptwin)

    for way in range(2):
        grad_arrived(1, 1, way)

    for stage in range(4):
        for piece in range(PIECES):
            dense(stage, piece).wait_send()
    for kind in range(3):
        for stage in range(2):
            for way in range(2):
                grad(kind, stage, way).wait_send()
    give.wait_send()
    for owner in range(SUBS):
        for which in range(2):
            mid_copy(owner, which).wait()


def finish_kernel(
    steps_s, dual_in, mid_weights, mid_sums, near, weights_out, sums_out, dual_out, terms, result, out_sem
):
    def out_copy(part, which):
        at = part * OUT_PART
        return pltpu.make_async_copy(
            result.at[which, pl.ds(at, OUT_PART)],
            (weights_out, sums_out)[which].at[pl.ds(at, OUT_PART)],
            out_sem.at[which, part],
        )

    dual_out[...] = dual_in[...]
    fill_terms(terms, near, True)
    ids1 = lane_ids(near, True)
    for part in range(OUT_PARTS):
        at = part * OUT_PART
        w = mid_weights[pl.ds(at, OUT_PART), :]
        gradient = PENALTY * w + onehot_sum(part_ids(at) == ids1, terms[...])
        s = mid_sums[pl.ds(at, OUT_PART), :] + gradient * gradient
        result[0, pl.ds(at, OUT_PART), :] = (
            w - primal_step(steps_s, 1, (OUT_PART, TILE)) * gradient / jnp.sqrt(s)
        )
        result[1, pl.ds(at, OUT_PART), :] = s
        for which in range(2):
            out_copy(part, which).start()
    for part in range(OUT_PARTS):
        for which in range(2):
            out_copy(part, which).wait()


def per_device(
    n, tile_values, tile_rows, tile_cols, tile_counts, labels, dual_logits, weights, adagrad_sums, section_steps
):
    any_space = pl.BlockSpec(memory_space=pl.ANY)
    smem = pl.BlockSpec(memory_space=pltpu.SMEM)
    vmem = pl.BlockSpec(memory_space=pltpu.VMEM)
    dma = pltpu.SemaphoreType.DMA
    dense_shape = jax.ShapeDtypeStruct((CTILES, TILE), F32)
    row_shape = jax.ShapeDtypeStruct((GROUP, TILE), F32)
    mid_weights, mid_sums, near1, dual = pl.pallas_call(
        functools.partial(kernel, n),
        out_shape=(dense_shape, dense_shape, jax.ShapeDtypeStruct((SUBS, CROWS, TILE), jnp.int16), row_shape),
        in_specs=[smem, smem, smem, smem, vmem, vmem, vmem, any_space, any_space, any_space],
        out_specs=(any_space, any_space, any_space, vmem),
        scratch_shapes=[
            pltpu.VMEM((2, SLOTS, TILE, TILE), BF16),
            pltpu.VMEM((CTILES, TILE), F32),
            pltpu.VMEM((CTILES, TILE), F32),
            pltpu.VMEM((1, SLOTS), I32),
            pltpu.SMEM((1, SLOTS), I32),
            pltpu.VMEM((2, SLOTS, TILE), F32),
            pltpu.VMEM((2, SLOTS, TILE), F32),
            pltpu.VMEM((SLOTS, TILE), F32),
            pltpu.VMEM((GROUP, TILE), F32),
            pltpu.VMEM((2, GROWS, TILE), F32),
            pltpu.VMEM((2, CROWS, TILE), jnp.int16),
            pltpu.VMEM((SUBS, GROWS, TILE), F32),
            pltpu.VMEM((SUBS, CROWS, TILE), jnp.int16),
            pltpu.VMEM((PIECES, 2, PIECE, TILE), jnp.int16),
            pltpu.VMEM((SUBS, PIECES, 2, PIECE, TILE), jnp.int16),
            pltpu.VMEM((SUBS * SLOTS, 2 * TILE), BF16),
            pltpu.VMEM((2, CTILES, TILE), F32),
            dma((2, max(LOADS))),
            dma((3,)),
            dma((2,)),
            dma((2,)),
            dma((4, PIECES)),
            dma((4, PIECES)),
            dma((3, 2, 2)),
            dma((3, 2, 2)),
            dma((2, OUT_PARTS)),
        ],
        compiler_params=pltpu.CompilerParams(
            collective_id=0, has_side_effects=True, vmem_limit_bytes=62 * 1024 * 1024
        ),
        name="descent",
    )(
        tile_rows.reshape(-1),
        tile_cols.reshape(-1),
        tile_counts.reshape(-1),
        section_steps,
        tile_cols,
        labels.reshape(GROUP, TILE),
        dual_logits.reshape(GROUP, TILE),
        tile_values,
        weights.reshape(CTILES, TILE),
        adagrad_sums.reshape(CTILES, TILE),
    )
    out = pl.pallas_call(
        finish_kernel,
        out_shape=(dense_shape, dense_shape, row_shape),
        in_specs=[smem, vmem, vmem, vmem, vmem],
        out_specs=(any_space, any_space, vmem),
        scratch_shapes=[
            pltpu.VMEM((SUBS * SLOTS, 2 * TILE), BF16),
            pltpu.VMEM((2, CTILES, TILE), F32),
            dma((2, OUT_PARTS)),
        ],
        compiler_params=pltpu.CompilerParams(vmem_limit_bytes=62 * 1024 * 1024),
        name="finish",
    )(section_steps, dual, mid_weights, mid_sums, near1)
    return out[0].reshape(-1), out[1].reshape(-1), out[2].reshape(-1)


def solution(mesh):
    in_specs = (
        P(None, ("blk", "sub"), None, None, None),
        P(None, ("blk", "sub"), None),
        P(None, ("blk", "sub"), None),
        P(None, ("blk", "sub")),
        P(("blk", "sub")),
        P(("blk", "sub")),
        P("blk"),
        P("blk"),
        P(),
    )
    out_specs = (P("blk"), P("blk"), P(("blk", "sub")))
    return jax.shard_map(
        functools.partial(per_device, mesh.shape["blk"]),
        mesh=mesh,
        in_specs=in_specs,
        out_specs=out_specs,
        check_vma=False,
    )
```

```python
import functools

import jax
import jax.numpy as jnp
from jax import lax
from jax.experimental import pallas as pl
from jax.experimental.pallas import tpu as pltpu
from jax.sharding import PartitionSpec as P

MESH = pl.DeviceIdType.MESH
SUBS = 4
SLOTS = 128
TILE = 128
GROUP = 16
GROUPS = SLOTS // GROUP
WIDE = 4
CTILES = 2048
QUARTER = CTILES // SUBS
PIECES = 2
PIECE = QUARTER // PIECES
GROWS = SLOTS + 8
CROWS = SLOTS + GROUP
OUT_PARTS = SUBS
OUT_PART = CTILES // OUT_PARTS
LOADS = (4, 2)

PENALTY = 0.1
DUAL_RATE = 0.5
PRIMAL_RATE = 0.8

LEVELS = 32766.0
WEIGHT_CODE = (-25.0, 27.6)
GRADIENT_CODE = (-18.0, 22.7)
SUM_MID = 0.275
SUM_SCALE = 32767.0 / 0.22501

F32 = jnp.float32
BF16 = jnp.bfloat16
I32 = jnp.int32


def encode_log(value, code_range):
    low, span = code_range
    size = jnp.log2(jnp.maximum(jnp.abs(value), 1e-30))
    code = jnp.clip(jnp.round((size - low) * (LEVELS / span)), 0.0, LEVELS)
    return jnp.where(value < 0.0, -code, code).astype(I32).astype(jnp.int16)


def decode_log(code, code_range):
    low, span = code_range
    code = code.astype(I32).astype(F32)
    size = jnp.exp2(jnp.abs(code) * (span / LEVELS) + low)
    return jnp.where(code < 0.0, -size, jnp.where(code > 0.0, size, 0.0))


def encode_sums(value):
    code = jnp.clip(jnp.round((value - SUM_MID) * SUM_SCALE), -32767.0, 32767.0)
    return code.astype(I32).astype(jnp.int16)


def decode_sums(code):
    return code.astype(I32).astype(F32) * (1.0 / SUM_SCALE) + SUM_MID


def split_terms(value):
    high = value.astype(BF16)
    low = (value - high.astype(F32)).astype(BF16)
    return jnp.concatenate([high, low], axis=1)


def onehot_sum(match, terms):
    both = jnp.dot(match.astype(F32).astype(BF16), terms, preferred_element_type=F32)
    return both[:, :TILE] + both[:, TILE:]


def fill_terms(terms, source, coded):
    for other in range(SUBS):
        value = source[other, :SLOTS, :]
        if coded:
            value = decode_log(value, GRADIENT_CODE)
        terms[pl.ds(other * SLOTS, SLOTS), :] = split_terms(value)


def lane_ids(source, coded):
    ids = [source[other, SLOTS:, :] for other in range(SUBS)]
    if coded:
        ids = [value.astype(I32).astype(F32) for value in ids]
    return jnp.concatenate([value[:1, :] for value in ids], axis=1)


def primal_step(steps_s, section, shape):
    steps = jnp.full(shape, steps_s[section], I32).astype(F32)
    return PRIMAL_RATE / jnp.sqrt(steps)


def part_ids(at):
    return (lax.broadcasted_iota(I32, (OUT_PART, SUBS * SLOTS), 0) + at).astype(F32)


def kernel(
    n,
    rows_s,
    cols_s,
    counts_s,
    steps_s,
    cols_v,
    labels_v,
    dual_v,
    tiles_h,
    weights_h,
    sums_h,
    mid_weights,
    mid_sums,
    near1,
    dual_out,
    tiles,
    weights,
    sums,
    asked_v,
    asked_s,
    answer,
    answered,
    answer_sums,
    answer_code,
    answered_code,
    hrows,
    scaled,
    grads,
    coded,
    near0,
    far0,
    quarter,
    codes,
    old,
    terms,
    result,
    tile_sem,
    local_sem,
    ask_sem,
    answer_sem,
    dense_send,
    dense_recv,
    grad_send,
    grad_recv,
    out_sem,
):
    p = lax.axis_index("blk")
    q = lax.axis_index("sub")
    twin = q + 1 - 2 * lax.rem(q, 2)
    opp = lax.rem(q + 2, SUBS)
    opptwin = lax.rem(twin + 2, SUBS)
    after = lax.rem(p + 1, n)
    after2 = lax.rem(p + 2, n)
    before = lax.rem(p + n - 1, n)
    before2 = lax.rem(p + n - 2, n)

    barrier = pltpu.get_barrier_semaphore()
    senders = [(before, q), (before, opp), (before2, q), (before2, opp), (after, q), (p, twin), (p, opp)]
    for device in senders:
        pl.semaphore_signal(barrier, inc=1, device_id=device, device_id_type=MESH)

    def tile_copy(section, load):
        size = SLOTS // LOADS[section]
        return pltpu.make_async_copy(
            tiles_h.at[section, 0, pl.ds(load * size, size)],
            tiles.at[section, pl.ds(load * size, size)],
            tile_sem.at[section, load],
        )

    def quarter_copy(which):
        at = pl.multiple_of(q * QUARTER, QUARTER)
        return pltpu.make_async_copy(
            (weights_h, sums_h)[which].at[pl.ds(at, QUARTER)], quarter.at[which], local_sem.at[3 + which]
        )

    for which in range(2):
        quarter_copy(which).start()
    copy_w = pltpu.make_async_copy(weights_h, weights, local_sem.at[0])
    copy_w.start()
    for load in range(LOADS[0]):
        tile_copy(0, load).start()
    copy_s = pltpu.make_async_copy(sums_h, sums, local_sem.at[1])
    copy_s.start()
    for load in range(LOADS[1]):
        tile_copy(1, load).start()

    def remote(src, dst, send, recv, device):
        return pltpu.make_async_remote_copy(
            src_ref=src, dst_ref=dst, send_sem=send, recv_sem=recv, device_id=device, device_id_type=MESH
        )

    sub16 = lax.broadcasted_iota(I32, (GROUP, TILE), 0)

    def forward(section, load_h):
        count = counts_s[section]
        base = section * SLOTS

        def group(g, total):
            for j in range(0, GROUP, WIDE):
                lhs = []
                for i in range(WIDE):
                    k = g * GROUP + j + i
                    row = jnp.where(k < count, rows_s[base + k], -1)
                    lhs.append(jnp.where(sub16 == row, load_h(k), 0.0).astype(BF16))
                rhs = [tiles[section, g * GROUP + j + i] for i in range(WIDE)]
                total = total + lax.dot_general(
                    jnp.concatenate(lhs, axis=1),
                    jnp.concatenate(rhs, axis=1),
                    (((1,), (1,)), ((), ())),
                    preferred_element_type=F32,
                )
            return total

        total = jnp.zeros((GROUP, TILE), F32)
        each = GROUPS // LOADS[section]
        for load in range(LOADS[section]):
            tile_copy(section, load).wait()
            total = lax.fori_loop(load * each, (load + 1) * each, group, total)
        return total

    def new_logits(section, logits, margins):
        steps = jnp.full((GROUP, TILE), steps_s[section], I32).astype(F32)
        dual_step = DUAL_RATE / jnp.sqrt(steps)
        signs = labels_v[...].astype(F32)
        logits = (1.0 - dual_step) * logits - dual_step * signs * margins
        scaled[...] = jax.nn.sigmoid(logits) * signs
        return logits

    def backward(section):
        count = counts_s[section]
        base = section * SLOTS

        def group(g, carry):
            lhs = []
            for j in range(GROUP):
                k = g * GROUP + j
                slot = jnp.where(k < count, j, -1)
                value = scaled[pl.ds(rows_s[base + k], 1), :]
                lhs.append(jnp.where(sub16 == slot, value, 0.0).astype(BF16))
            rhs = tiles[section, pl.ds(g * GROUP, GROUP)].reshape(GROUP * TILE, TILE)
            grads[section, pl.ds(pl.multiple_of(g * GROUP, GROUP), GROUP), :] = jnp.dot(
                jnp.concatenate(lhs, axis=1), rhs, preferred_element_type=F32
            )
            return carry

        lax.fori_loop(0, GROUPS, group, 0)

    ask = remote(cols_v.at[1], asked_v, ask_sem.at[0], ask_sem.at[1], (before, q))

    def dense(stage, piece):
        owner = opp if stage == 3 else q
        to = ((after2, q), (p, opp), (p, twin), (p, twin))[stage]
        src = codes.at[piece] if stage == 0 else old.at[owner, piece]
        return remote(src, old.at[owner, piece], dense_send.at[stage, piece], dense_recv.at[stage, piece], to)

    def dense_arrived(stage, piece):
        ref = old.at[(q, opp, twin, opptwin)[stage], piece]
        remote(ref, ref, dense_send.at[stage, piece], dense_recv.at[stage, piece], (p, twin)).wait_recv()

    def grad(kind, stage, way):
        target = (near0, near1, far0)[kind]
        owner = (q, opp)[way]
        if stage == 0:
            src, slot = (grads.at[0], coded.at[1], coded.at[0])[kind], q
            to = ((after, after, after2)[kind], owner)
        else:
            src, slot = target.at[owner], owner
            to = (p, twin)
        return remote(
            src, target.at[slot], grad_send.at[kind, stage, way], grad_recv.at[kind, stage, way], to
        )

    def grad_arrived(kind, stage, way):
        target = (near0, near1, far0)[kind]
        owner = ((q, opp), (twin, opptwin))[stage][way]
        ref = target.at[owner]
        remote(
            ref, ref, grad_send.at[kind, stage, way], grad_recv.at[kind, stage, way], (p, twin)
        ).wait_recv()

    grads[0, pl.ds(SLOTS, 8), :] = jnp.broadcast_to(cols_v[0].astype(F32), (8, TILE))
    for section in range(2):
        coded[section, pl.ds(SLOTS, GROUP), :] = jnp.broadcast_to(cols_v[section], (GROUP, TILE)).astype(
            jnp.int16
        )

    for which in range(2):
        quarter_copy(which).wait()
    for piece in range(PIECES):
        codes[piece, 0] = encode_log(quarter[0, pl.ds(piece * PIECE, PIECE), :], WEIGHT_CODE)
        codes[piece, 1] = encode_sums(quarter[1, pl.ds(piece * PIECE, PIECE), :])
    pl.semaphore_wait(barrier, len(senders))
    ask.start()
    dense(0, 0).start()
    dense(0, 1).start()
    copy_w.wait()
    margins = forward(0, lambda k: weights[pl.ds(cols_s[k], 1), :])
    logits = new_logits(0, dual_v[...], margins)

    copy_s.wait()
    backward(0)
    for way in range(2):
        grad(0, 0, way).start()

    coded[0, :SLOTS, :] = encode_log(grads[0, :SLOTS, :], GRADIENT_CODE)

    ask.wait()
    to_scalar = pltpu.make_async_copy(asked_v, asked_s, local_sem.at[2])
    to_scalar.start()
    to_scalar.wait()

    def gather(g, carry):
        for j in range(GROUP):
            k = g * GROUP + j
            at = asked_s[0, k]
            answer[pl.ds(k, 1), :] = weights[pl.ds(at, 1), :]
            answer_sums[pl.ds(k, 1), :] = sums[pl.ds(at, 1), :]
        return carry

    lax.fori_loop(0, GROUPS, gather, 0)
    answer_code[...] = encode_sums(answer_sums[...])
    give = remote(answer, answered, answer_sem.at[0], answer_sem.at[1], (after, q))
    give.start()
    give_sums = remote(answer_code, answered_code, answer_sem.at[2], answer_sem.at[3], (after, q))
    give_sums.start()

    dense_arrived(0, 0)
    dense(1, 0).start()
    dense(2, 0).start()
    mine = jnp.transpose(jnp.broadcast_to(cols_v[1].astype(F32), (TILE, TILE)))
    mine = jnp.concatenate([mine] * SUBS, axis=1)
    for way in range(2):
        grad_arrived(0, 0, way)
        grad(0, 1, way).start()
    dense_arrived(0, 1)
    dense(1, 1).start()
    dense(2, 1).start()
    give.wait_recv()
    give_sums.wait_recv()
    answered_sums = decode_sums(answered_code[...])
    for way in range(2):
        grad_arrived(0, 1, way)
    for way in range(2):
        grad(2, 0, way).start()
    fill_terms(terms, near0, False)
    picked = onehot_sum(mine == lane_ids(near0, False), terms[...])
    gradient = PENALTY * answered[...] + picked
    after_sums = answered_sums + gradient * gradient
    hrows[...] = answered[...] - primal_step(steps_s, 0, (SLOTS, TILE)) * gradient / jnp.sqrt(after_sums)

    margins = forward(1, lambda k: hrows[pl.ds(k, 1), :])
    logits = new_logits(1, logits, margins)
    dual_out[...] = logits
    backward(1)
    coded[1, :SLOTS, :] = encode_log(grads[1, :SLOTS, :], GRADIENT_CODE)
    for way in range(2):
        grad(1, 0, way).start()

    for way in range(2):
        grad_arrived(2, 0, way)
        grad(2, 1, way).start()
    dense_arrived(1, 0)
    dense(3, 0).start()
    for way in range(2):
        grad_arrived(2, 1, way)
    fill_terms(terms, far0, True)
    ids0 = lane_ids(far0, True)

    def mid_copy(owner, which):
        at = pl.multiple_of(owner * OUT_PART, OUT_PART)
        return pltpu.make_async_copy(
            result.at[which, pl.ds(at, OUT_PART)],
            (mid_weights, mid_sums)[which].at[pl.ds(at, OUT_PART)],
            out_sem.at[which, owner],
        )

    def section0(owner):
        at = pl.multiple_of(owner * OUT_PART, OUT_PART)
        w = decode_log(old[owner, :, 0].reshape(OUT_PART, TILE), WEIGHT_CODE)
        s = decode_sums(old[owner, :, 1].reshape(OUT_PART, TILE))
        gradient = PENALTY * w + onehot_sum(part_ids(at) == ids0, terms[...])
        s = s + gradient * gradient
        result[0, pl.ds(at, OUT_PART), :] = (
            w - primal_step(steps_s, 0, (OUT_PART, TILE)) * gradient / jnp.sqrt(s)
        )
        result[1, pl.ds(at, OUT_PART), :] = s
        for which in range(2):
            mid_copy(owner, which).start()

    section0(q)
    for piece in range(PIECES):
        dense_arrived(2, piece)
    section0(twin)
    for piece in range(1, PIECES):
        dense_arrived(1, piece)
        dense(3, piece).start()
    for way in range(2):
        grad_arrived(1, 0, way)
        grad(1, 1, way).start()
    section0(opp)
    for piece in range(PIECES):
        dense_arrived(3, piece)
    section0(opptwin)

    for way in range(2):
        grad_arrived(1, 1, way)

    for stage in range(4):
        for piece in range(PIECES):
            dense(stage, piece).wait_send()
    for kind in range(3):
        for stage in range(2):
            for way in range(2):
                grad(kind, stage, way).wait_send()
    give.wait_send()
    give_sums.wait_send()
    for owner in range(SUBS):
        for which in range(2):
            mid_copy(owner, which).wait()


def finish_kernel(
    steps_s, dual_in, mid_weights, mid_sums, near, weights_out, sums_out, dual_out, terms, result, out_sem
):
    def out_copy(part, which):
        at = part * OUT_PART
        return pltpu.make_async_copy(
            result.at[which, pl.ds(at, OUT_PART)],
            (weights_out, sums_out)[which].at[pl.ds(at, OUT_PART)],
            out_sem.at[which, part],
        )

    dual_out[...] = dual_in[...]
    fill_terms(terms, near, True)
    ids1 = lane_ids(near, True)
    for part in range(OUT_PARTS):
        at = part * OUT_PART
        w = mid_weights[pl.ds(at, OUT_PART), :]
        gradient = PENALTY * w + onehot_sum(part_ids(at) == ids1, terms[...])
        s = mid_sums[pl.ds(at, OUT_PART), :] + gradient * gradient
        result[0, pl.ds(at, OUT_PART), :] = (
            w - primal_step(steps_s, 1, (OUT_PART, TILE)) * gradient / jnp.sqrt(s)
        )
        result[1, pl.ds(at, OUT_PART), :] = s
        for which in range(2):
            out_copy(part, which).start()
    for part in range(OUT_PARTS):
        for which in range(2):
            out_copy(part, which).wait()


def per_device(
    n, tile_values, tile_rows, tile_cols, tile_counts, labels, dual_logits, weights, adagrad_sums, section_steps
):
    any_space = pl.BlockSpec(memory_space=pl.ANY)
    smem = pl.BlockSpec(memory_space=pltpu.SMEM)
    vmem = pl.BlockSpec(memory_space=pltpu.VMEM)
    dma = pltpu.SemaphoreType.DMA
    dense_shape = jax.ShapeDtypeStruct((CTILES, TILE), F32)
    row_shape = jax.ShapeDtypeStruct((GROUP, TILE), F32)
    mid_weights, mid_sums, near1, dual = pl.pallas_call(
        functools.partial(kernel, n),
        out_shape=(dense_shape, dense_shape, jax.ShapeDtypeStruct((SUBS, CROWS, TILE), jnp.int16), row_shape),
        in_specs=[smem, smem, smem, smem, vmem, vmem, vmem, any_space, any_space, any_space],
        out_specs=(any_space, any_space, any_space, vmem),
        scratch_shapes=[
            pltpu.VMEM((2, SLOTS, TILE, TILE), BF16),
            pltpu.VMEM((CTILES, TILE), F32),
            pltpu.VMEM((CTILES, TILE), F32),
            pltpu.VMEM((1, SLOTS), I32),
            pltpu.SMEM((1, SLOTS), I32),
            pltpu.VMEM((SLOTS, TILE), F32),
            pltpu.VMEM((SLOTS, TILE), F32),
            pltpu.VMEM((SLOTS, TILE), F32),
            pltpu.VMEM((SLOTS, TILE), jnp.int16),
            pltpu.VMEM((SLOTS, TILE), jnp.int16),
            pltpu.VMEM((SLOTS, TILE), F32),
            pltpu.VMEM((GROUP, TILE), F32),
            pltpu.VMEM((2, GROWS, TILE), F32),
            pltpu.VMEM((2, CROWS, TILE), jnp.int16),
            pltpu.VMEM((SUBS, GROWS, TILE), F32),
            pltpu.VMEM((SUBS, CROWS, TILE), jnp.int16),
            pltpu.VMEM((2, QUARTER, TILE), F32),
            pltpu.VMEM((PIECES, 2, PIECE, TILE), jnp.int16),
            pltpu.VMEM((SUBS, PIECES, 2, PIECE, TILE), jnp.int16),
            pltpu.VMEM((SUBS * SLOTS, 2 * TILE), BF16),
            pltpu.VMEM((2, CTILES, TILE), F32),
            dma((2, max(LOADS))),
            dma((5,)),
            dma((2,)),
            dma((4,)),
            dma((4, PIECES)),
            dma((4, PIECES)),
            dma((3, 2, 2)),
            dma((3, 2, 2)),
            dma((2, OUT_PARTS)),
        ],
        compiler_params=pltpu.CompilerParams(
            collective_id=0, has_side_effects=True, vmem_limit_bytes=62 * 1024 * 1024
        ),
        name="descent",
    )(
        tile_rows.reshape(-1),
        tile_cols.reshape(-1),
        tile_counts.reshape(-1),
        section_steps,
        tile_cols,
        labels.reshape(GROUP, TILE),
        dual_logits.reshape(GROUP, TILE),
        tile_values,
        weights.reshape(CTILES, TILE),
        adagrad_sums.reshape(CTILES, TILE),
    )
    out = pl.pallas_call(
        finish_kernel,
        out_shape=(dense_shape, dense_shape, row_shape),
        in_specs=[smem, vmem, vmem, vmem, vmem],
        out_specs=(any_space, any_space, vmem),
        scratch_shapes=[
            pltpu.VMEM((SUBS * SLOTS, 2 * TILE), BF16),
            pltpu.VMEM((2, CTILES, TILE), F32),
            dma((2, OUT_PARTS)),
        ],
        compiler_params=pltpu.CompilerParams(vmem_limit_bytes=62 * 1024 * 1024),
        name="finish",
    )(section_steps, dual, mid_weights, mid_sums, near1)
    return out[0].reshape(-1), out[1].reshape(-1), out[2].reshape(-1)


def solution(mesh):
    in_specs = (
        P(None, ("blk", "sub"), None, None, None),
        P(None, ("blk", "sub"), None),
        P(None, ("blk", "sub"), None),
        P(None, ("blk", "sub")),
        P(("blk", "sub")),
        P(("blk", "sub")),
        P("blk"),
        P("blk"),
        P(),
    )
    out_specs = (P("blk"), P("blk"), P(("blk", "sub")))
    return jax.shard_map(
        functools.partial(per_device, mesh.shape["blk"]),
        mesh=mesh,
        in_specs=in_specs,
        out_specs=out_specs,
        check_vma=False,
    )
```

```python
import functools

import jax
import jax.numpy as jnp
from jax import lax
from jax.experimental import pallas as pl
from jax.experimental.pallas import tpu as pltpu
from jax.sharding import PartitionSpec as P

MESH = pl.DeviceIdType.MESH
SUBS = 4
SLOTS = 128
TILE = 128
GROUP = 16
GROUPS = SLOTS // GROUP
WIDE = 4
CTILES = 2048
QUARTER = CTILES // SUBS
PIECES = 2
PIECE = QUARTER // PIECES
GROWS = SLOTS + 8
CROWS = SLOTS + GROUP
OUT_PARTS = SUBS
OUT_PART = CTILES // OUT_PARTS
LOADS = (4, 1)

PENALTY = 0.1
DUAL_RATE = 0.5
PRIMAL_RATE = 0.8

LEVELS = 32766.0
WEIGHT_CODE = (-25.0, 27.6)
GRADIENT_CODE = (-18.0, 22.7)
SUM_MID = 0.275
SUM_SCALE = 32767.0 / 0.22501

F32 = jnp.float32
BF16 = jnp.bfloat16
I32 = jnp.int32


def encode_log(value, code_range):
    low, span = code_range
    size = jnp.log2(jnp.maximum(jnp.abs(value), 1e-30))
    code = jnp.clip(jnp.round((size - low) * (LEVELS / span)), 0.0, LEVELS)
    return jnp.where(value < 0.0, -code, code).astype(I32).astype(jnp.int16)


def decode_log(code, code_range):
    low, span = code_range
    code = code.astype(I32).astype(F32)
    size = jnp.exp2(jnp.abs(code) * (span / LEVELS) + low)
    return jnp.where(code < 0.0, -size, jnp.where(code > 0.0, size, 0.0))


def encode_sums(value):
    code = jnp.clip(jnp.round((value - SUM_MID) * SUM_SCALE), -32767.0, 32767.0)
    return code.astype(I32).astype(jnp.int16)


def decode_sums(code):
    return code.astype(I32).astype(F32) * (1.0 / SUM_SCALE) + SUM_MID


def split_terms(value):
    high = value.astype(BF16)
    low = (value - high.astype(F32)).astype(BF16)
    return jnp.concatenate([high, low], axis=1)


def onehot_sum(match, terms):
    both = jnp.dot(match.astype(F32).astype(BF16), terms, preferred_element_type=F32)
    return both[:, :TILE] + both[:, TILE:]


def fill_terms(terms, source, coded):
    for other in range(SUBS):
        value = source[other, :SLOTS, :]
        if coded:
            value = decode_log(value, GRADIENT_CODE)
        terms[pl.ds(other * SLOTS, SLOTS), :] = split_terms(value)


def lane_ids(source, coded):
    ids = [source[other, SLOTS:, :] for other in range(SUBS)]
    if coded:
        ids = [value.astype(I32).astype(F32) for value in ids]
    return jnp.concatenate([value[:1, :] for value in ids], axis=1)


def primal_step(steps_s, section, shape):
    steps = jnp.full(shape, steps_s[section], I32).astype(F32)
    return PRIMAL_RATE / jnp.sqrt(steps)


def part_ids(at):
    return (lax.broadcasted_iota(I32, (OUT_PART, SUBS * SLOTS), 0) + at).astype(F32)


def kernel(
    n,
    rows_s,
    cols_s,
    counts_s,
    steps_s,
    cols_v,
    labels_v,
    dual_v,
    tiles_h,
    weights_h,
    sums_h,
    mid_weights,
    mid_sums,
    near1,
    dual_out,
    tiles,
    weights,
    sums,
    asked_v,
    asked_s,
    answer,
    answered,
    answer_sums,
    answer_code,
    answered_code,
    hrows,
    scaled,
    grads,
    coded,
    near0,
    far0,
    quarter,
    codes,
    old,
    terms,
    result,
    tile_sem,
    local_sem,
    ask_sem,
    answer_sem,
    dense_send,
    dense_recv,
    grad_send,
    grad_recv,
    last_send,
    last_recv,
    out_sem,
):
    p = lax.axis_index("blk")
    q = lax.axis_index("sub")
    twin = q + 1 - 2 * lax.rem(q, 2)
    opp = lax.rem(q + 2, SUBS)
    opptwin = lax.rem(twin + 2, SUBS)
    after = lax.rem(p + 1, n)
    after2 = lax.rem(p + 2, n)
    before = lax.rem(p + n - 1, n)
    before2 = lax.rem(p + n - 2, n)

    barrier = pltpu.get_barrier_semaphore()
    senders = [(before, q), (before, opp), (before, twin), (before, opptwin), (before2, q), (before2, opp), (after, q), (p, twin), (p, opp)]
    for device in senders:
        pl.semaphore_signal(barrier, inc=1, device_id=device, device_id_type=MESH)

    def tile_copy(section, load):
        size = SLOTS // LOADS[section]
        return pltpu.make_async_copy(
            tiles_h.at[section, 0, pl.ds(load * size, size)],
            tiles.at[section, pl.ds(load * size, size)],
            tile_sem.at[section, load],
        )

    def quarter_copy(which):
        at = pl.multiple_of(q * QUARTER, QUARTER)
        return pltpu.make_async_copy(
            (weights_h, sums_h)[which].at[pl.ds(at, QUARTER)], quarter.at[which], local_sem.at[3 + which]
        )

    for which in range(2):
        quarter_copy(which).start()
    copy_w = pltpu.make_async_copy(weights_h, weights, local_sem.at[0])
    copy_w.start()
    for load in range(LOADS[0]):
        tile_copy(0, load).start()
    copy_s = pltpu.make_async_copy(sums_h, sums, local_sem.at[1])
    copy_s.start()
    for load in range(LOADS[1]):
        tile_copy(1, load).start()

    def remote(src, dst, send, recv, device):
        return pltpu.make_async_remote_copy(
            src_ref=src, dst_ref=dst, send_sem=send, recv_sem=recv, device_id=device, device_id_type=MESH
        )

    sub16 = lax.broadcasted_iota(I32, (GROUP, TILE), 0)

    def forward(section, load_h):
        count = counts_s[section]
        base = section * SLOTS

        def group(g, total):
            for j in range(0, GROUP, WIDE):
                lhs = []
                for i in range(WIDE):
                    k = g * GROUP + j + i
                    row = jnp.where(k < count, rows_s[base + k], -1)
                    lhs.append(jnp.where(sub16 == row, load_h(k), 0.0).astype(BF16))
                rhs = [tiles[section, g * GROUP + j + i] for i in range(WIDE)]
                total = total + lax.dot_general(
                    jnp.concatenate(lhs, axis=1),
                    jnp.concatenate(rhs, axis=1),
                    (((1,), (1,)), ((), ())),
                    preferred_element_type=F32,
                )
            return total

        total = jnp.zeros((GROUP, TILE), F32)
        each = GROUPS // LOADS[section]
        for load in range(LOADS[section]):
            tile_copy(section, load).wait()
            total = lax.fori_loop(load * each, (load + 1) * each, group, total)
        return total

    def new_logits(section, logits, margins):
        steps = jnp.full((GROUP, TILE), steps_s[section], I32).astype(F32)
        dual_step = DUAL_RATE / jnp.sqrt(steps)
        signs = labels_v[...].astype(F32)
        logits = (1.0 - dual_step) * logits - dual_step * signs * margins
        scaled[...] = jax.nn.sigmoid(logits) * signs
        return logits

    def backward(section):
        count = counts_s[section]
        base = section * SLOTS

        def group(g, carry):
            lhs = []
            for j in range(GROUP):
                k = g * GROUP + j
                slot = jnp.where(k < count, j, -1)
                value = scaled[pl.ds(rows_s[base + k], 1), :]
                lhs.append(jnp.where(sub16 == slot, value, 0.0).astype(BF16))
            rhs = tiles[section, pl.ds(g * GROUP, GROUP)].reshape(GROUP * TILE, TILE)
            grads[section, pl.ds(pl.multiple_of(g * GROUP, GROUP), GROUP), :] = jnp.dot(
                jnp.concatenate(lhs, axis=1), rhs, preferred_element_type=F32
            )
            return carry

        lax.fori_loop(0, GROUPS, group, 0)

    ask = remote(cols_v.at[1], asked_v, ask_sem.at[0], ask_sem.at[1], (before, q))

    def dense(stage, piece):
        owner = opp if stage == 3 else q
        to = ((after2, q), (p, opp), (p, twin), (p, twin))[stage]
        src = codes.at[piece] if stage == 0 else old.at[owner, piece]
        return remote(src, old.at[owner, piece], dense_send.at[stage, piece], dense_recv.at[stage, piece], to)

    def dense_arrived(stage, piece):
        ref = old.at[(q, opp, twin, opptwin)[stage], piece]
        remote(ref, ref, dense_send.at[stage, piece], dense_recv.at[stage, piece], (p, twin)).wait_recv()

    def grad(kind, stage, way):
        target = (near0, near1, far0)[kind]
        owner = (q, opp)[way]
        if stage == 0:
            src, slot = (grads.at[0], coded.at[1], coded.at[0])[kind], q
            to = ((after, after, after2)[kind], owner)
        else:
            src, slot = target.at[owner], owner
            to = (p, twin)
        return remote(
            src, target.at[slot], grad_send.at[kind, stage, way], grad_recv.at[kind, stage, way], to
        )

    def grad_arrived(kind, stage, way):
        target = (near0, near1, far0)[kind]
        owner = ((q, opp), (twin, opptwin))[stage][way]
        ref = target.at[owner]
        remote(
            ref, ref, grad_send.at[kind, stage, way], grad_recv.at[kind, stage, way], (p, twin)
        ).wait_recv()

    def last(turn):
        to = (q, opp, twin, opptwin)[turn]
        return remote(
            coded.at[1], near1.at[q], last_send.at[turn], last_recv.at[turn], (after, to)
        )

    def last_arrived(turn):
        ref = near1.at[(q, opp, twin, opptwin)[turn]]
        remote(ref, ref, last_send.at[turn], last_recv.at[turn], (p, twin)).wait_recv()

    grads[0, pl.ds(SLOTS, 8), :] = jnp.broadcast_to(cols_v[0].astype(F32), (8, TILE))
    for section in range(2):
        coded[section, pl.ds(SLOTS, GROUP), :] = jnp.broadcast_to(cols_v[section], (GROUP, TILE)).astype(
            jnp.int16
        )

    for which in range(2):
        quarter_copy(which).wait()
    def encode(piece):
        codes[piece, 0] = encode_log(quarter[0, pl.ds(piece * PIECE, PIECE), :], WEIGHT_CODE)
        codes[piece, 1] = encode_sums(quarter[1, pl.ds(piece * PIECE, PIECE), :])

    encode(0)
    pl.semaphore_wait(barrier, len(senders))
    ask.start()
    dense(0, 0).start()
    encode(1)
    dense(0, 1).start()
    copy_w.wait()
    margins = forward(0, lambda k: weights[pl.ds(cols_s[k], 1), :])
    logits = new_logits(0, dual_v[...], margins)

    copy_s.wait()
    backward(0)
    for way in range(2):
        grad(0, 0, way).start()
    coded[0, :SLOTS, :] = encode_log(grads[0, :SLOTS, :], GRADIENT_CODE)
    for way in range(2):
        grad(2, 0, way).start()


    ask.wait()
    to_scalar = pltpu.make_async_copy(asked_v, asked_s, local_sem.at[2])
    to_scalar.start()
    to_scalar.wait()

    def gather(g, carry):
        for j in range(GROUP):
            k = g * GROUP + j
            at = asked_s[0, k]
            answer[pl.ds(k, 1), :] = weights[pl.ds(at, 1), :]
            answer_sums[pl.ds(k, 1), :] = sums[pl.ds(at, 1), :]
        return carry

    lax.fori_loop(0, GROUPS, gather, 0)
    answer_code[...] = encode_sums(answer_sums[...])
    give = remote(answer, answered, answer_sem.at[0], answer_sem.at[1], (after, q))
    give.start()
    give_sums = remote(answer_code, answered_code, answer_sem.at[2], answer_sem.at[3], (after, q))
    give_sums.start()

    dense_arrived(0, 0)
    dense(1, 0).start()
    dense(2, 0).start()
    mine = jnp.transpose(jnp.broadcast_to(cols_v[1].astype(F32), (TILE, TILE)))
    mine = jnp.concatenate([mine] * SUBS, axis=1)
    for way in range(2):
        grad_arrived(0, 0, way)
        grad(0, 1, way).start()
    dense_arrived(0, 1)
    dense(1, 1).start()
    dense(2, 1).start()
    give.wait_recv()
    give_sums.wait_recv()
    answered_sums = decode_sums(answered_code[...])
    for way in range(2):
        grad_arrived(0, 1, way)
    fill_terms(terms, near0, False)
    picked = onehot_sum(mine == lane_ids(near0, False), terms[...])
    gradient = PENALTY * answered[...] + picked
    after_sums = answered_sums + gradient * gradient
    hrows[...] = answered[...] - primal_step(steps_s, 0, (SLOTS, TILE)) * gradient / jnp.sqrt(after_sums)

    margins = forward(1, lambda k: hrows[pl.ds(k, 1), :])
    logits = new_logits(1, logits, margins)
    dual_out[...] = logits
    for way in range(2):
        grad_arrived(2, 0, way)
        grad(2, 1, way).start()
    backward(1)
    coded[1, :SLOTS, :] = encode_log(grads[1, :SLOTS, :], GRADIENT_CODE)
    for turn in range(SUBS):
        last(turn).start()

    dense_arrived(1, 0)
    dense(3, 0).start()
    for way in range(2):
        grad_arrived(2, 1, way)
    fill_terms(terms, far0, True)
    ids0 = lane_ids(far0, True)

    def mid_copy(owner, which):
        at = pl.multiple_of(owner * OUT_PART, OUT_PART)
        return pltpu.make_async_copy(
            result.at[which, pl.ds(at, OUT_PART)],
            (mid_weights, mid_sums)[which].at[pl.ds(at, OUT_PART)],
            out_sem.at[which, owner],
        )

    def section0(owner):
        at = pl.multiple_of(owner * OUT_PART, OUT_PART)
        w = decode_log(old[owner, :, 0].reshape(OUT_PART, TILE), WEIGHT_CODE)
        s = decode_sums(old[owner, :, 1].reshape(OUT_PART, TILE))
        gradient = PENALTY * w + onehot_sum(part_ids(at) == ids0, terms[...])
        s = s + gradient * gradient
        result[0, pl.ds(at, OUT_PART), :] = (
            w - primal_step(steps_s, 0, (OUT_PART, TILE)) * gradient / jnp.sqrt(s)
        )
        result[1, pl.ds(at, OUT_PART), :] = s
        for which in range(2):
            mid_copy(owner, which).start()

    section0(q)
    for piece in range(PIECES):
        dense_arrived(2, piece)
    section0(twin)
    for piece in range(1, PIECES):
        dense_arrived(1, piece)
        dense(3, piece).start()
    section0(opp)
    for piece in range(PIECES):
        dense_arrived(3, piece)
    section0(opptwin)

    for stage in range(4):
        for piece in range(PIECES):
            dense(stage, piece).wait_send()
    for kind in (0, 2):
        for stage in range(2):
            for way in range(2):
                grad(kind, stage, way).wait_send()
    give.wait_send()
    give_sums.wait_send()
    for turn in range(SUBS):
        last(turn).wait_send()
    for owner in range(SUBS):
        for which in range(2):
            mid_copy(owner, which).wait()
    for turn in range(SUBS):
        last_arrived(turn)


def finish_kernel(
    steps_s, dual_in, mid_weights, mid_sums, near, weights_out, sums_out, dual_out, terms, result, out_sem
):
    def out_copy(part, which):
        at = part * OUT_PART
        return pltpu.make_async_copy(
            result.at[which, pl.ds(at, OUT_PART)],
            (weights_out, sums_out)[which].at[pl.ds(at, OUT_PART)],
            out_sem.at[which, part],
        )

    dual_out[...] = dual_in[...]
    fill_terms(terms, near, True)
    ids1 = lane_ids(near, True)
    for part in range(OUT_PARTS):
        at = part * OUT_PART
        w = mid_weights[pl.ds(at, OUT_PART), :]
        gradient = PENALTY * w + onehot_sum(part_ids(at) == ids1, terms[...])
        s = mid_sums[pl.ds(at, OUT_PART), :] + gradient * gradient
        result[0, pl.ds(at, OUT_PART), :] = (
            w - primal_step(steps_s, 1, (OUT_PART, TILE)) * gradient / jnp.sqrt(s)
        )
        result[1, pl.ds(at, OUT_PART), :] = s
        for which in range(2):
            out_copy(part, which).start()
    for part in range(OUT_PARTS):
        for which in range(2):
            out_copy(part, which).wait()


def per_device(
    n, tile_values, tile_rows, tile_cols, tile_counts, labels, dual_logits, weights, adagrad_sums, section_steps
):
    any_space = pl.BlockSpec(memory_space=pl.ANY)
    smem = pl.BlockSpec(memory_space=pltpu.SMEM)
    vmem = pl.BlockSpec(memory_space=pltpu.VMEM)
    dma = pltpu.SemaphoreType.DMA
    dense_shape = jax.ShapeDtypeStruct((CTILES, TILE), F32)
    row_shape = jax.ShapeDtypeStruct((GROUP, TILE), F32)
    mid_weights, mid_sums, near1, dual = pl.pallas_call(
        functools.partial(kernel, n),
        out_shape=(dense_shape, dense_shape, jax.ShapeDtypeStruct((SUBS, CROWS, TILE), jnp.int16), row_shape),
        in_specs=[smem, smem, smem, smem, vmem, vmem, vmem, any_space, any_space, any_space],
        out_specs=(any_space, any_space, any_space, vmem),
        scratch_shapes=[
            pltpu.VMEM((2, SLOTS, TILE, TILE), BF16),
            pltpu.VMEM((CTILES, TILE), F32),
            pltpu.VMEM((CTILES, TILE), F32),
            pltpu.VMEM((1, SLOTS), I32),
            pltpu.SMEM((1, SLOTS), I32),
            pltpu.VMEM((SLOTS, TILE), F32),
            pltpu.VMEM((SLOTS, TILE), F32),
            pltpu.VMEM((SLOTS, TILE), F32),
            pltpu.VMEM((SLOTS, TILE), jnp.int16),
            pltpu.VMEM((SLOTS, TILE), jnp.int16),
            pltpu.VMEM((SLOTS, TILE), F32),
            pltpu.VMEM((GROUP, TILE), F32),
            pltpu.VMEM((2, GROWS, TILE), F32),
            pltpu.VMEM((2, CROWS, TILE), jnp.int16),
            pltpu.VMEM((SUBS, GROWS, TILE), F32),
            pltpu.VMEM((SUBS, CROWS, TILE), jnp.int16),
            pltpu.VMEM((2, QUARTER, TILE), F32),
            pltpu.VMEM((PIECES, 2, PIECE, TILE), jnp.int16),
            pltpu.VMEM((SUBS, PIECES, 2, PIECE, TILE), jnp.int16),
            pltpu.VMEM((SUBS * SLOTS, 2 * TILE), BF16),
            pltpu.VMEM((2, CTILES, TILE), F32),
            dma((2, max(LOADS))),
            dma((5,)),
            dma((2,)),
            dma((4,)),
            dma((4, PIECES)),
            dma((4, PIECES)),
            dma((3, 2, 2)),
            dma((3, 2, 2)),
            dma((SUBS,)),
            dma((SUBS,)),
            dma((2, OUT_PARTS)),
        ],
        compiler_params=pltpu.CompilerParams(
            collective_id=0, has_side_effects=True, vmem_limit_bytes=62 * 1024 * 1024
        ),
        name="descent",
    )(
        tile_rows.reshape(-1),
        tile_cols.reshape(-1),
        tile_counts.reshape(-1),
        section_steps,
        tile_cols,
        labels.reshape(GROUP, TILE),
        dual_logits.reshape(GROUP, TILE),
        tile_values,
        weights.reshape(CTILES, TILE),
        adagrad_sums.reshape(CTILES, TILE),
    )
    out = pl.pallas_call(
        finish_kernel,
        out_shape=(dense_shape, dense_shape, row_shape),
        in_specs=[smem, vmem, vmem, vmem, vmem],
        out_specs=(any_space, any_space, vmem),
        scratch_shapes=[
            pltpu.VMEM((SUBS * SLOTS, 2 * TILE), BF16),
            pltpu.VMEM((2, CTILES, TILE), F32),
            dma((2, OUT_PARTS)),
        ],
        compiler_params=pltpu.CompilerParams(vmem_limit_bytes=62 * 1024 * 1024),
        name="finish",
    )(section_steps, dual, mid_weights, mid_sums, near1)
    return out[0].reshape(-1), out[1].reshape(-1), out[2].reshape(-1)


def solution(mesh):
    in_specs = (
        P(None, ("blk", "sub"), None, None, None),
        P(None, ("blk", "sub"), None),
        P(None, ("blk", "sub"), None),
        P(None, ("blk", "sub")),
        P(("blk", "sub")),
        P(("blk", "sub")),
        P("blk"),
        P("blk"),
        P(),
    )
    out_specs = (P("blk"), P("blk"), P(("blk", "sub")))
    return jax.shard_map(
        functools.partial(per_device, mesh.shape["blk"]),
        mesh=mesh,
        in_specs=in_specs,
        out_specs=out_specs,
        check_vma=False,
    )
```
